32 devices in a mesh: ta: 8 (over y, x, core), xy: 4 (over z).
Axes of the slice: x: 2, y: 2, z: 4, core: 2. Of those that a mesh axis runs over, the one named last changes fastest.
Arguments:
- residual: bfloat16 [8, 32, 2, 2, 12, 128], P('ta', 'xy'), may hold values from -6 to 6
- vectors: bfloat16 [8, 8, 1, 2, 2, 24, 3072], P('ta', 'xy'), may hold values from -0.625 to 0.625
- hopping: bfloat16 [8, 2, 24, 24, 8, 8, 1, 2], P(None, None, None, None, 'ta', 'xy'), may hold values from -0.3125 to 0.3125
- inverse: bfloat16 [2, 24, 24, 8, 8, 1, 2], P(None, None, None, 'ta', 'xy'), may hold values from -0.41 to 1.81
Outputs:
- correction: float32 [8, 32, 2, 2, 12, 128], P('ta', 'xy')
The draws below stay inside these ranges and needn't reach their ends.
All inputs are finite; a program needn't handle non-finite values.
Results may differ from the reference program's by a relative error of at most 0.0029.
Values may be sent and summed in bfloat16 or wider, within the bound.
A program may use at most 64 MiB of HBM per device.

```python
import jax
import jax.numpy as jnp
from jax import lax

NVEC = 24
FINE = 3072
NRHS = 2
CZQ = 1
CY = 2
CT = 2
CZG = 4
CXG = 8
TF = 8
XF = 32
ZYF = 128
N_TA = 8


def draw_inverse(key, part):
    key = jax.random.fold_in(key, 7)
    first_key, second_key = jax.random.split(key)
    shape = (2, NVEC, NVEC, N_TA, CXG, CZQ, CY)
    jitter = 0.1 * jax.random.truncated_normal(first_key, -4.0, 4.0, shape, jnp.float32)
    diagonal = jax.random.uniform(second_key, (NVEC, N_TA, CXG, CZQ, CY), jnp.float32, 0.6, 1.4)
    identity = jnp.eye(NVEC, dtype=jnp.float32)[:, :, None, None, None, None]
    real_part = jitter[0] + identity * diagonal[:, None]
    return jnp.stack((real_part, jitter[1])).astype(jnp.bfloat16)


def block_scale(stream_key, dims, cuts, low, largest):
    def one(position, parts):
        draws = jax.random.uniform(jax.random.fold_in(jax.random.fold_in(stream_key, 6), position), (parts,), jnp.float32, low / len(cuts), largest / len(cuts))
        return jnp.repeat(jnp.exp(draws), dims[position] // parts).reshape((-1,) + (1,) * (len(dims) - position - 1))

    factor_of = one(*cuts[0])
    for cut in cuts[1:]:
        factor_of = factor_of * one(*cut)
    return factor_of


def centred(rng, extent, width, limit, cuts=(), kind=jnp.bfloat16):
    factor_of = block_scale(rng, extent, cuts, -0.22, 0.18) if cuts else 1.0
    result = jax.random.normal(rng, extent, jnp.float32) * width * factor_of
    return jnp.minimum(jnp.maximum(result, -limit), limit).astype(kind)


def setup_inputs(seed: int = 0) -> dict:
    streams_of = jax.random.split(jax.random.key(seed), 5)
    residual = centred(streams_of[0], (TF, XF, NRHS, 2, 12, ZYF), 1.0, 6.0, ((0, 8), (1, 4)))
    vectors = centred(streams_of[1], (N_TA, CXG, CZQ, CY, 2, NVEC, FINE), ((4 * FINE * NVEC) ** -0.25), 0.625, ((0, 8), (1, 4)))
    hopping = centred(streams_of[2], (8, 2, NVEC, NVEC, N_TA, CXG, CZQ, CY), (0.4 / (16 * NVEC) ** 0.5), 0.3125, ((4, 8), (5, 4)))
    inverse = draw_inverse(jax.random.fold_in(streams_of[4], 71), 0)
    return dict(residual=residual, vectors=vectors, hopping=hopping, inverse=inverse)


highest = lax.Precision.HIGHEST


def to_lattice(values):
    trailing = values.shape[4:]
    shaped = values.reshape((CT, 4, CXG, CZQ, CY) + trailing)
    shaped = jnp.moveaxis(shaped, 3, 2)
    return shaped.reshape((CT, CZG, CXG, CY) + trailing)


def from_lattice(values):
    trailing = values.shape[4:]
    shaped = values.reshape((CT, 4, CZQ, CXG, CY) + trailing)
    shaped = jnp.moveaxis(shaped, 2, 3)
    return shaped.reshape((N_TA, CXG, CZQ, CY) + trailing)


def complex_apply(matrix, vector_field):
    products = jnp.einsum('...pab,...rqb->...rpqa', matrix, vector_field, precision=highest)
    real_part = products[..., 0, 0, :] - products[..., 1, 1, :]
    imag_part = products[..., 0, 1, :] + products[..., 1, 0, :]
    return jnp.stack((real_part, imag_part), axis=-2)


def hopping_term(link_blocks, vector_field):
    summed = jnp.zeros_like(vector_field)
    for direction in range(8):
        axis_of = direction // 2
        roll_step = -1 if direction % 2 == 0 else 1
        shifted = jnp.roll(vector_field, roll_step, axis=axis_of)
        summed = summed + complex_apply(link_blocks[..., direction, :, :, :], shifted)
    return summed


def restrict_row(row_pair):
    vector_row, field_row = row_pair
    products = jnp.einsum('abcpkf,abcrqf->abcrpqk', vector_row.astype(jnp.float32), field_row.astype(jnp.float32), precision=highest)
    real_part = products[..., 0, 0, :] + products[..., 1, 1, :]
    imag_part = products[..., 0, 1, :] - products[..., 1, 0, :]
    return jnp.stack((real_part, imag_part), axis=-2)


def prolong_row(row_pair):
    vector_row, coarse_row = row_pair
    products = jnp.einsum('abcpkf,abcrqk->abcrpqf', vector_row.astype(jnp.float32), coarse_row.astype(jnp.float32), precision=highest)
    real_part = products[:, :, :, :, 0, 0] - products[:, :, :, :, 1, 1]
    imag_part = products[:, :, :, :, 0, 1] + products[:, :, :, :, 1, 0]
    return jnp.stack((real_part, imag_part), axis=4)


def reference(residual, vectors, hopping, inverse):
    fine_rows = residual.reshape(CT, 4, CXG, 4, NRHS, 2, 12, 4, CZQ, 4, CY, 4)
    fine_rows = fine_rows.transpose(0, 7, 2, 8, 10, 4, 5, 6, 1, 9, 3, 11)
    fine_rows = fine_rows.reshape(N_TA, CXG, CZQ, CY, NRHS, 2, FINE)
    coarse_rhs = to_lattice(lax.map(restrict_row, (vectors, fine_rows)))
    link_blocks = to_lattice(jnp.moveaxis(hopping, (4, 5, 6, 7), (0, 1, 2, 3)).astype(jnp.float32))
    blocks = to_lattice(jnp.moveaxis(inverse, (3, 4, 5, 6), (0, 1, 2, 3)).astype(jnp.float32))
    solution = complex_apply(blocks, coarse_rhs)
    for sweep_index in range(2):
        solution = complex_apply(blocks, coarse_rhs - hopping_term(link_blocks, solution))
    rounded = from_lattice(solution).astype(jnp.bfloat16)
    spread_rows = lax.map(prolong_row, (vectors, rounded))
    spread_rows = spread_rows.reshape(CT, 4, CXG, CZQ, CY, NRHS, 2, 12, 4, 4, 4, 4)
    spread_rows = spread_rows.transpose(0, 8, 2, 10, 5, 6, 7, 1, 3, 9, 4, 11)
    return spread_rows.reshape(TF, XF, NRHS, 2, 12, ZYF)
```

```python
import functools

import jax
import jax.numpy as jnp
from jax import lax
from jax.experimental import pallas as pl
from jax.experimental.pallas import tpu as pltpu
from jax.sharding import PartitionSpec as P

F32 = jnp.float32
BF16 = jnp.bfloat16
NT = (((1,), (1,)), ((), ()))
MESH = pl.DeviceIdType.MESH


def dot(a, b):
    return jnp.dot(a, b, preferred_element_type=F32)


def dot_nt(a, b):
    return lax.dot_general(a, b, NT, preferred_element_type=F32)


def lanes(rows):
    return lax.broadcasted_iota(jnp.int32, (rows, 128), 1)


def ahead(x, by):
    return pltpu.roll(x, 128 - by, 1)


def behind(x, by):
    return pltpu.roll(x, by, 1)


def swap(x, lane, bit):
    return jnp.where((lane & bit) == 0, ahead(x, bit), behind(x, bit))


def times_i(x, lane):
    return jnp.where((lane & 4) == 0, -ahead(x, 4), behind(x, 4))


def own_site(x_of_site, lane):
    site = (lane & 2) + ((lane >> 3) & 1)
    total = jnp.where(site == 0, x_of_site(0), 0.0)
    for s in range(1, 4):
        total = total + jnp.where(site == s, x_of_site(s), 0.0)
    return total


def spread_groups(x):
    for by in (64, 32, 16):
        x = x + pltpu.roll(x, by, 1)
    return x


def split_field(v, lane):
    high = v.astype(BF16).astype(F32)
    base = jnp.where((lane & 16) == 0, high, v - high)
    return jnp.where((lane & 32) == 0, base, times_i(base, lane))


def pad_rows(w):
    return jnp.concatenate([w, jnp.zeros((8, 128), F32)], axis=0).astype(BF16)


def kernel(
    n_ta,
    n_xy,
    res_hbm,
    vec_hbm,
    hop_hbm,
    inv_hbm,
    out_ref,
    res,
    vec,
    hop,
    inv,
    perm,
    send_in,
    recv_in,
    halo_out,
    halo_in,
    send_back,
    recv_back,
    rows_ref,
    load_sem,
    in_send,
    in_recv,
    halo_send,
    halo_recv,
    back_send,
    back_recv,
):
    ta = lax.axis_index("ta")
    xy = lax.axis_index("xy")
    q = ta % 4
    base = ta - q
    n_t = n_ta // 4

    loads = []
    for i, (src, dst) in enumerate(((res_hbm, res), (vec_hbm, vec), (hop_hbm, hop), (inv_hbm, inv))):
        copy = pltpu.make_async_copy(src, dst, load_sem.at[i])
        copy.start()
        loads.append(copy)

    t_up = (ta + 4) % n_ta
    t_down = (ta + n_ta - 4) % n_ta
    x_up = (xy + 1) % n_xy
    x_down = (xy + n_xy - 1) % n_xy
    mates = [base + (q + j) % 4 for j in (1, 2, 3)]
    greeted = [(mate, xy) for mate in mates] + [(ta, x_up), (ta, x_down), (t_up, xy)]
    if n_t > 2:
        greeted.append((t_down, xy))
    barrier = pltpu.get_barrier_semaphore()
    for device in greeted:
        pl.semaphore_signal(barrier, inc=1, device_id=device, device_id_type=MESH)

    row128 = lax.broadcasted_iota(jnp.int32, (128, 128), 0)
    col128 = lanes(128)
    target = (row128 >> 5) * 128 + ((row128 >> 2) & 1) * 64 + ((row128 >> 3) & 3) * 16 + (row128 & 3)
    offset = target - col128
    for xi in range(4):
        for zq in range(4):
            perm[128 * xi : 128 * xi + 128, 128 * zq : 128 * zq + 128] = jnp.where(
                offset == 128 * zq - 4 * xi, 1.0, 0.0
            ).astype(BF16)
    r96 = lax.broadcasted_iota(jnp.int32, (96, 96), 0)
    c96 = lax.broadcasted_iota(jnp.int32, (96, 96), 1)

    def fine_row(i):
        return ((i >> 1) & 1) * 48 + (i & 1) * 24 + (i >> 3) * 2 + ((i >> 2) & 1)

    gather = jnp.where(c96 == fine_row(r96), 1.0, 0.0).astype(BF16)
    scatter = jnp.where(r96 == fine_row(c96), 1.0, 0.0).astype(BF16)

    loads[0].wait()
    wide = jnp.concatenate(
        [
            jnp.concatenate([res[4 * xc + xi] for xi in range(4)], axis=1)
            for xc in range(2)
        ],
        axis=0,
    )
    sorted_rows = dot(wide, perm[...]).astype(BF16)
    for zq in range(4):
        send_in[zq] = sorted_rows[:, 128 * zq : 128 * zq + 128]

    pl.semaphore_wait(barrier, len(greeted))

    def exchange(src, dst, send_sem, recv_sem):
        copies = []
        for j in (2, 3, 1):
            slot = (q + j) % 4
            copy = pltpu.make_async_remote_copy(
                src_ref=src.at[slot],
                dst_ref=dst.at[q],
                send_sem=send_sem.at[j - 1],
                recv_sem=recv_sem.at[j - 1],
                device_id=(base + slot, xy),
                device_id_type=MESH,
            )
            copy.start()
            copies.append(copy)
        dst[pl.ds(q, 1)] = src[pl.ds(q, 1)]
        return copies

    copies_in = exchange(send_in, recv_in, in_send, in_recv)
    loads[1].wait()
    loads[2].wait()
    loads[3].wait()
    for copy in copies_in:
        copy.wait()

    lane96 = lanes(96)
    lane24 = lanes(24)
    low96 = lane96 < 64
    gathered = [dot(gather, recv_in[ti]) for ti in range(4)]
    turned = [pltpu.roll(g, 64, 1) for g in gathered]
    halves = []
    for yc in range(2):
        blocks = []
        for h in range(2):
            if yc == 0:
                blocks.append(jnp.where(low96, gathered[2 * h], turned[2 * h + 1]))
            else:
                blocks.append(jnp.where(low96, turned[2 * h], gathered[2 * h + 1]))
        halves.append(
            jnp.concatenate(
                [blocks[h][8 * c : 8 * c + 8] for c in range(12) for h in range(2)], axis=1
            )
        )
    fine = jnp.concatenate(halves, axis=0).astype(BF16)
    fine = jnp.concatenate([fine] * 8, axis=0)
    products = dot_nt(vec[...], fine)

    def part_of(p):
        return own_site(lambda s: products[24 * (2 * s + p) : 24 * (2 * s + p) + 24], lane24)

    rhs = part_of(0) - times_i(part_of(1), lane24)

    def collapse(acc, keep):
        picked = jnp.where((lane96 & 32) == 0, acc[:96], acc[96:])
        if keep:
            picked = jnp.where(low96, picked, 0.0)
        rows_ref[...] = picked
        return spread_groups(own_site(lambda s: rows_ref[pl.ds(s, 24, stride=4)], lane24))

    def apply_block(u):
        w = split_field(u, lane24).astype(BF16)
        return collapse(dot(inv[...], w), True)

    solution = apply_block(rhs)
    for sweep in range(2):
        plain = split_field(solution, lane24)
        w = jnp.where(lane24 < 64, plain, swap(plain, lane24, 2))
        halo_out[sweep] = pad_rows(w)
        copies = {}
        routes = [(5, (ta, x_up)), (4, (ta, x_down)), (0, (t_down, xy))]
        if n_t > 2:
            routes.append((1, (t_up, xy)))
        routes += [(2, (base + (q + 3) % 4, xy)), (3, (base + (q + 1) % 4, xy))]
        for slot, device in routes:
            copy = pltpu.make_async_remote_copy(
                src_ref=halo_out.at[sweep],
                dst_ref=halo_in.at[sweep, slot],
                send_sem=halo_send.at[sweep, slot],
                recv_sem=halo_recv.at[sweep, slot],
                device_id=device,
                device_id_type=MESH,
            )
            copy.start()
            copies[slot] = copy
        flipped = swap(plain, lane24, 8).astype(BF16)
        acc = dot(hop[6], flipped) + dot(hop[7], flipped)
        for mu in (2, 3, 0, 1):
            slot = 0 if mu == 1 and n_t == 2 else mu
            if slot == mu:
                copies[slot].wait_recv()
            acc = acc + dot(hop[mu], halo_in[sweep, slot][:24])
        copies[4].wait_recv()
        copies[5].wait_recv()
        first_x = (lane24 & 2) == 0
        above = jnp.where(first_x, w, halo_in[sweep, 4][:24].astype(F32)).astype(BF16)
        below = jnp.where(first_x, halo_in[sweep, 5][:24].astype(F32), w).astype(BF16)
        acc_x = dot(hop[4], above) + dot(hop[5], below)
        acc = jnp.where(lanes(192) < 64, acc, acc_x)
        solution = apply_block(rhs - collapse(acc, False))
        for copy in copies.values():
            copy.wait_send()

    rounded = solution.astype(BF16).astype(F32)
    rotated = times_i(rounded, lane24)
    site = (lane24 & 2) + ((lane24 >> 3) & 1)
    columns = jnp.concatenate(
        [jnp.where(site == s, part, 0.0) for s in range(4) for part in (rounded, rotated)], axis=0
    ).astype(BF16)
    pick = (lax.broadcasted_iota(jnp.int32, (16, 128), 0) == lanes(16)).astype(F32).astype(BF16)
    coefficients = dot_nt(pick, columns).astype(BF16)
    spread = dot(coefficients, vec[...])
    for h in range(2):
        straight = []
        for yc in range(2):
            straight.append(
                jnp.concatenate(
                    [
                        spread[8 * yc : 8 * yc + 8, 256 * c + 128 * h : 256 * c + 128 * h + 128]
                        for c in range(12)
                    ],
                    axis=0,
                )
            )
        crossed = [pltpu.roll(s, 64, 1) for s in straight]
        send_back[2 * h] = jnp.where(low96, straight[0], crossed[1]).astype(BF16)
        send_back[2 * h + 1] = jnp.where(low96, crossed[0], straight[1]).astype(BF16)
    for copy in exchange(send_back, recv_back, back_send, back_recv):
        copy.wait()
    returned = jnp.concatenate(
        [dot(scatter, recv_back[zq]).astype(BF16) for zq in range(4)], axis=1
    )
    result = dot_nt(returned, perm[...])
    for xc in range(2):
        for xi in range(4):
            out_ref[4 * xc + xi] = result[48 * xc : 48 * xc + 48, 128 * xi : 128 * xi + 128]


def shards(n_ta, n_xy, residual, vectors, hopping, inverse):
    res = residual[0].transpose(0, 1, 3, 2, 4).reshape(8, 48, 128)
    vec = vectors.reshape(192, 3072)
    hop = hopping[:, :, :, :, 0, :, 0, :].transpose(0, 1, 2, 4, 5, 3).reshape(8, 192, 24)
    inv = inverse[:, :, :, 0, :, 0, :].transpose(0, 1, 3, 4, 2).reshape(192, 24)
    out = pl.pallas_call(
        functools.partial(kernel, n_ta, n_xy),
        out_shape=jax.ShapeDtypeStruct((8, 48, 128), F32),
        in_specs=[pl.BlockSpec(memory_space=pl.ANY)] * 4,
        out_specs=pl.BlockSpec(memory_space=pltpu.VMEM),
        scratch_shapes=[
            pltpu.VMEM((8, 48, 128), BF16),
            pltpu.VMEM((192, 3072), BF16),
            pltpu.VMEM((8, 192, 24), BF16),
            pltpu.VMEM((192, 24), BF16),
            pltpu.VMEM((512, 512), BF16),
            pltpu.VMEM((4, 96, 128), BF16),
            pltpu.VMEM((4, 96, 128), BF16),
            pltpu.VMEM((2, 32, 128), BF16),
            pltpu.VMEM((2, 6, 32, 128), BF16),
            pltpu.VMEM((4, 96, 128), BF16),
            pltpu.VMEM((4, 96, 128), BF16),
            pltpu.VMEM((96, 128), F32),
            pltpu.SemaphoreType.DMA((4,)),
            pltpu.SemaphoreType.DMA((3,)),
            pltpu.SemaphoreType.DMA((3,)),
            pltpu.SemaphoreType.DMA((2, 6)),
            pltpu.SemaphoreType.DMA((2, 6)),
            pltpu.SemaphoreType.DMA((3,)),
            pltpu.SemaphoreType.DMA((3,)),
        ],
        compiler_params=pltpu.CompilerParams(
            collective_id=0, has_side_effects=True, vmem_limit_bytes=32 * 1024 * 1024
        ),
    )(res, vec, hop, inv)
    return out.reshape(1, 8, 2, 12, 2, 128).transpose(0, 1, 2, 4, 3, 5)


def solution(mesh):
    placed = (
        P("ta", "xy", None, None, None, None),
        P("ta", "xy", None, None, None, None, None),
        P(None, None, None, None, "ta", "xy", None, None),
        P(None, None, None, "ta", "xy", None, None),
    )
    return jax.shard_map(
        functools.partial(shards, mesh.shape["ta"], mesh.shape["xy"]),
        mesh=mesh,
        in_specs=placed,
        out_specs=P("ta", "xy", None, None, None, None),
        check_vma=False,
    )
```

```python
import functools

import jax
import jax.numpy as jnp
from jax import lax
from jax.experimental import pallas as pl
from jax.experimental.pallas import tpu as pltpu
from jax.sharding import PartitionSpec as P

F32 = jnp.float32
BF16 = jnp.bfloat16
NT = (((1,), (1,)), ((), ()))
MESH = pl.DeviceIdType.MESH


def dot(a, b):
    return jnp.dot(a, b, preferred_element_type=F32)


def dot_nt(a, b):
    return lax.dot_general(a, b, NT, preferred_element_type=F32)


def lanes(rows):
    return lax.broadcasted_iota(jnp.int32, (rows, 128), 1)


def ahead(x, by):
    return pltpu.roll(x, 128 - by, 1)


def behind(x, by):
    return pltpu.roll(x, by, 1)


def swap(x, lane, bit):
    return jnp.where((lane & bit) == 0, ahead(x, bit), behind(x, bit))


def times_i(x, lane):
    return jnp.where((lane & 4) == 0, -ahead(x, 4), behind(x, 4))


def own_site(x_of_site, lane):
    site = (lane & 2) + ((lane >> 3) & 1)
    total = jnp.where(site == 0, x_of_site(0), 0.0)
    for s in range(1, 4):
        total = total + jnp.where(site == s, x_of_site(s), 0.0)
    return total


def spread_groups(x):
    for by in (64, 32, 16):
        x = x + pltpu.roll(x, by, 1)
    return x


def split_field(v, lane):
    high = v.astype(BF16).astype(F32)
    base = jnp.where((lane & 16) == 0, high, v - high)
    return jnp.where((lane & 32) == 0, base, times_i(base, lane))


def pad_rows(w):
    return jnp.concatenate([w, jnp.zeros((8, 128), F32)], axis=0).astype(BF16)


def kernel(
    n_ta,
    n_xy,
    res_hbm,
    vec_hbm,
    hop_hbm,
    inv_hbm,
    out_ref,
    res,
    vec,
    hop,
    inv,
    perm,
    send_in,
    recv_in,
    halo_out,
    halo_in,
    send_back,
    recv_back,
    rows_ref,
    load_sem,
    in_send,
    in_recv,
    halo_send,
    halo_recv,
    back_send,
    back_recv,
):
    ta = lax.axis_index("ta")
    xy = lax.axis_index("xy")
    q = ta % 4
    base = ta - q
    n_t = n_ta // 4

    loads = []
    for i, (src, dst) in enumerate(((res_hbm, res), (vec_hbm, vec), (hop_hbm, hop), (inv_hbm, inv))):
        copy = pltpu.make_async_copy(src, dst, load_sem.at[i])
        copy.start()
        loads.append(copy)

    t_up = (ta + 4) % n_ta
    t_down = (ta + n_ta - 4) % n_ta
    x_up = (xy + 1) % n_xy
    x_down = (xy + n_xy - 1) % n_xy
    mates = [base + (q + j) % 4 for j in (1, 2, 3)]
    greeted = [(mate, xy) for mate in mates] + [(ta, x_up), (ta, x_down), (t_up, xy)]
    if n_t > 2:
        greeted.append((t_down, xy))
    barrier = pltpu.get_barrier_semaphore()
    for device in greeted:
        pl.semaphore_signal(barrier, inc=1, device_id=device, device_id_type=MESH)

    row128 = lax.broadcasted_iota(jnp.int32, (128, 128), 0)
    col128 = lanes(128)
    target = (row128 >> 5) * 128 + ((row128 >> 2) & 1) * 64 + ((row128 >> 3) & 3) * 16 + (row128 & 3)
    offset = target - col128
    for xi in range(4):
        for zq in range(4):
            perm[128 * xi : 128 * xi + 128, 128 * zq : 128 * zq + 128] = jnp.where(
                offset == 128 * zq - 4 * xi, 1.0, 0.0
            ).astype(BF16)
    r96 = lax.broadcasted_iota(jnp.int32, (96, 96), 0)
    c96 = lax.broadcasted_iota(jnp.int32, (96, 96), 1)

    def fine_row(i):
        return ((i >> 1) & 1) * 48 + (i & 1) * 24 + (i >> 3) * 2 + ((i >> 2) & 1)

    gather = jnp.where(c96 == fine_row(r96), 1.0, 0.0).astype(BF16)
    scatter = jnp.where(r96 == fine_row(c96), 1.0, 0.0).astype(BF16)

    loads[0].wait()
    wide = jnp.concatenate(
        [
            jnp.concatenate([res[4 * xc + xi] for xi in range(4)], axis=1)
            for xc in range(2)
        ],
        axis=0,
    )
    sorted_rows = dot(wide, perm[...]).astype(BF16)
    for zq in range(4):
        send_in[zq] = sorted_rows[:, 128 * zq : 128 * zq + 128]

    pl.semaphore_wait(barrier, len(greeted))

    def exchange(src, dst, send_sem, recv_sem):
        copies = []
        for j in (2, 3, 1):
            slot = (q + j) % 4
            copy = pltpu.make_async_remote_copy(
                src_ref=src.at[slot],
                dst_ref=dst.at[q],
                send_sem=send_sem.at[j - 1],
                recv_sem=recv_sem.at[j - 1],
                device_id=(base + slot, xy),
                device_id_type=MESH,
            )
            copy.start()
            copies.append(copy)
        dst[pl.ds(q, 1)] = src[pl.ds(q, 1)]
        return copies

    copies_in = exchange(send_in, recv_in, in_send, in_recv)
    loads[1].wait()
    loads[2].wait()
    loads[3].wait()
    for copy in copies_in:
        copy.wait()

    lane96 = lanes(96)
    lane24 = lanes(24)
    low96 = lane96 < 64
    gathered = [dot(gather, recv_in[ti]) for ti in range(4)]
    turned = [pltpu.roll(g, 64, 1) for g in gathered]
    halves = []
    for yc in range(2):
        blocks = []
        for h in range(2):
            if yc == 0:
                blocks.append(jnp.where(low96, gathered[2 * h], turned[2 * h + 1]))
            else:
                blocks.append(jnp.where(low96, turned[2 * h], gathered[2 * h + 1]))
        halves.append(
            jnp.concatenate(
                [blocks[h][8 * c : 8 * c + 8] for c in range(12) for h in range(2)], axis=1
            )
        )
    fine = jnp.concatenate(halves, axis=0).astype(BF16)
    fine = jnp.concatenate([fine] * 8, axis=0)
    products = dot_nt(vec[...], fine)

    def part_of(p):
        return own_site(lambda s: products[24 * (2 * s + p) : 24 * (2 * s + p) + 24], lane24)

    rhs = part_of(0) - times_i(part_of(1), lane24)

    def collapse(acc, keep):
        picked = jnp.where((lane96 & 32) == 0, acc[:96], acc[96:])
        if keep:
            picked = jnp.where(low96, picked, 0.0)
        rows_ref[...] = picked
        return spread_groups(own_site(lambda s: rows_ref[pl.ds(s, 24, stride=4)], lane24))

    def apply_block(u):
        w = split_field(u, lane24).astype(BF16)
        return collapse(dot(inv[...], w), True)

    solution = apply_block(rhs)
    for sweep in range(2):
        plain = split_field(solution, lane24)
        w = jnp.where(lane24 < 64, plain, swap(plain, lane24, 2))
        halo_out[sweep] = pad_rows(w)
        copies = {}
        routes = [(5, (ta, x_up)), (4, (ta, x_down)), (0, (t_down, xy))]
        if n_t > 2:
            routes.append((1, (t_up, xy)))
        routes += [(2, (base + (q + 3) % 4, xy)), (3, (base + (q + 1) % 4, xy))]
        for slot, device in routes:
            copy = pltpu.make_async_remote_copy(
                src_ref=halo_out.at[sweep],
                dst_ref=halo_in.at[sweep, slot],
                send_sem=halo_send.at[sweep, slot],
                recv_sem=halo_recv.at[sweep, slot],
                device_id=device,
                device_id_type=MESH,
            )
            copy.start()
            copies[slot] = copy
        flipped = swap(plain, lane24, 8).astype(BF16)
        acc = dot(hop[6], flipped) + dot(hop[7], flipped)
        for mu in (2, 3, 0, 1):
            slot = 0 if mu == 1 and n_t == 2 else mu
            if slot == mu:
                copies[slot].wait_recv()
            acc = acc + dot(hop[mu], halo_in[sweep, slot][:24])
        copies[4].wait_recv()
        copies[5].wait_recv()
        first_x = (lane24 & 2) == 0
        above = jnp.where(first_x, w, halo_in[sweep, 4][:24].astype(F32)).astype(BF16)
        below = jnp.where(first_x, halo_in[sweep, 5][:24].astype(F32), w).astype(BF16)
        acc_x = dot(hop[4], above) + dot(hop[5], below)
        acc = jnp.where(lanes(192) < 64, acc, acc_x)
        solution = apply_block(rhs - collapse(acc, False))
        for copy in copies.values():
            copy.wait_send()

    rounded = solution.astype(BF16).astype(F32)
    rotated = times_i(rounded, lane24)
    site = (lane24 & 2) + ((lane24 >> 3) & 1)
    columns = jnp.concatenate(
        [jnp.where(site == s, part, 0.0) for s in range(4) for part in (rounded, rotated)], axis=0
    ).astype(BF16)
    pick = (lax.broadcasted_iota(jnp.int32, (16, 128), 0) == lanes(16)).astype(F32).astype(BF16)
    coefficients = dot_nt(pick, columns).astype(BF16)
    spread = dot(coefficients, vec[...])
    for h in range(2):
        straight = []
        for yc in range(2):
            straight.append(
                jnp.concatenate(
                    [
                        spread[8 * yc : 8 * yc + 8, 256 * c + 128 * h : 256 * c + 128 * h + 128]
                        for c in range(12)
                    ],
                    axis=0,
                )
            )
        crossed = [pltpu.roll(s, 64, 1) for s in straight]
        send_back[2 * h] = jnp.where(low96, straight[0], crossed[1]).astype(BF16)
        send_back[2 * h + 1] = jnp.where(low96, crossed[0], straight[1]).astype(BF16)
    for copy in exchange(send_back, recv_back, back_send, back_recv):
        copy.wait()
    returned = jnp.concatenate(
        [dot(scatter, recv_back[zq]).astype(BF16) for zq in range(4)], axis=1
    )
    result = dot_nt(returned, perm[...])
    for xc in range(2):
        for xi in range(4):
            out_ref[4 * xc + xi] = result[48 * xc : 48 * xc + 48, 128 * xi : 128 * xi + 128]


def shards(n_ta, n_xy, residual, vectors, hopping, inverse):
    res = residual[0].transpose(0, 1, 3, 2, 4).reshape(8, 48, 128)
    vec = vectors.reshape(192, 3072)
    hop = hopping[:, :, :, :, 0, :, 0, :].transpose(0, 1, 2, 4, 5, 3).reshape(8, 192, 24)
    inv = inverse[:, :, :, 0, :, 0, :].transpose(0, 1, 3, 4, 2).reshape(192, 24)
    out = pl.pallas_call(
        functools.partial(kernel, n_ta, n_xy),
        out_shape=jax.ShapeDtypeStruct((8, 48, 128), F32),
        in_specs=[pl.BlockSpec(memory_space=pltpu.HBM)] * 4,
        out_specs=pl.BlockSpec(memory_space=pltpu.VMEM),
        scratch_shapes=[
            pltpu.VMEM((8, 48, 128), BF16),
            pltpu.VMEM((192, 3072), BF16),
            pltpu.VMEM((8, 192, 24), BF16),
            pltpu.VMEM((192, 24), BF16),
            pltpu.VMEM((512, 512), BF16),
            pltpu.VMEM((4, 96, 128), BF16),
            pltpu.VMEM((4, 96, 128), BF16),
            pltpu.VMEM((2, 32, 128), BF16),
            pltpu.VMEM((2, 6, 32, 128), BF16),
            pltpu.VMEM((4, 96, 128), BF16),
            pltpu.VMEM((4, 96, 128), BF16),
            pltpu.VMEM((96, 128), F32),
            pltpu.SemaphoreType.DMA((4,)),
            pltpu.SemaphoreType.DMA((3,)),
            pltpu.SemaphoreType.DMA((3,)),
            pltpu.SemaphoreType.DMA((2, 6)),
            pltpu.SemaphoreType.DMA((2, 6)),
            pltpu.SemaphoreType.DMA((3,)),
            pltpu.SemaphoreType.DMA((3,)),
        ],
        compiler_params=pltpu.CompilerParams(
            collective_id=0, has_side_effects=True, vmem_limit_bytes=63 * 1024 * 1024
        ),
    )(res, vec, hop, inv)
    return out.reshape(1, 8, 2, 12, 2, 128).transpose(0, 1, 2, 4, 3, 5)


def solution(mesh):
    placed = (
        P("ta", "xy", None, None, None, None),
        P("ta", "xy", None, None, None, None, None),
        P(None, None, None, None, "ta", "xy", None, None),
        P(None, None, None, "ta", "xy", None, None),
    )
    return jax.shard_map(
        functools.partial(shards, mesh.shape["ta"], mesh.shape["xy"]),
        mesh=mesh,
        in_specs=placed,
        out_specs=P("ta", "xy", None, None, None, None),
        check_vma=False,
    )
```

```python
import functools

import jax
import jax.numpy as jnp
from jax import lax
from jax.experimental import pallas as pl
from jax.experimental.pallas import tpu as pltpu
from jax.sharding import PartitionSpec as P

F32 = jnp.float32
BF16 = jnp.bfloat16
NT = (((1,), (1,)), ((), ()))
MESH = pl.DeviceIdType.MESH


def dot(a, b):
    return jnp.dot(a, b, preferred_element_type=F32)


def dot_nt(a, b):
    return lax.dot_general(a, b, NT, preferred_element_type=F32)


def lanes(rows):
    return lax.broadcasted_iota(jnp.int32, (rows, 128), 1)


def ahead(x, by):
    return pltpu.roll(x, 128 - by, 1)


def behind(x, by):
    return pltpu.roll(x, by, 1)


def swap(x, lane, bit):
    return jnp.where((lane & bit) == 0, ahead(x, bit), behind(x, bit))


def times_i(x, lane):
    return jnp.where((lane & 4) == 0, -ahead(x, 4), behind(x, 4))


def own_site(x_of_site, lane):
    site = (lane & 2) + ((lane >> 3) & 1)
    total = jnp.where(site == 0, x_of_site(0), 0.0)
    for s in range(1, 4):
        total = total + jnp.where(site == s, x_of_site(s), 0.0)
    return total


def spread_groups(x):
    for by in (64, 32, 16):
        x = x + pltpu.roll(x, by, 1)
    return x


def split_field(v, lane):
    high = v.astype(BF16).astype(F32)
    base = jnp.where((lane & 16) == 0, high, v - high)
    return jnp.where((lane & 32) == 0, base, times_i(base, lane))


def pad_rows(w):
    return jnp.concatenate([w, jnp.zeros((8, 128), F32)], axis=0).astype(BF16)


def kernel(
    n_ta,
    n_xy,
    res_hbm,
    vec_hbm,
    hop_hbm,
    inv_hbm,
    out_ref,
    res,
    vec,
    hop,
    inv,
    perm,
    send_in,
    recv_in,
    halo_out,
    halo_in,
    send_back,
    recv_back,
    links,
    rows_ref,
    load_sem,
    in_send,
    in_recv,
    halo_send,
    halo_recv,
    back_send,
    back_recv,
):
    ta = lax.axis_index("ta")
    xy = lax.axis_index("xy")
    q = ta % 4
    base = ta - q
    n_t = n_ta // 4

    loads = []
    for i, (src, dst) in enumerate(((res_hbm, res), (vec_hbm, vec), (hop_hbm, hop), (inv_hbm, inv))):
        copy = pltpu.make_async_copy(src, dst, load_sem.at[i])
        copy.start()
        loads.append(copy)

    t_up = (ta + 4) % n_ta
    t_down = (ta + n_ta - 4) % n_ta
    x_up = (xy + 1) % n_xy
    x_down = (xy + n_xy - 1) % n_xy
    mates = [base + (q + j) % 4 for j in (1, 2, 3)]
    greeted = [(mate, xy) for mate in mates] + [(ta, x_up), (ta, x_down), (t_up, xy)]
    if n_t > 2:
        greeted.append((t_down, xy))
    barrier = pltpu.get_barrier_semaphore()
    for device in greeted:
        pl.semaphore_signal(barrier, inc=1, device_id=device, device_id_type=MESH)

    row128 = lax.broadcasted_iota(jnp.int32, (128, 128), 0)
    col128 = lanes(128)
    target = (row128 >> 5) * 128 + ((row128 >> 2) & 1) * 64 + ((row128 >> 3) & 3) * 16 + (row128 & 3)
    offset = target - col128
    for xi in range(4):
        for zq in range(4):
            perm[128 * xi : 128 * xi + 128, 128 * zq : 128 * zq + 128] = jnp.where(
                offset == 128 * zq - 4 * xi, 1.0, 0.0
            ).astype(BF16)
    r96 = lax.broadcasted_iota(jnp.int32, (96, 96), 0)
    c96 = lax.broadcasted_iota(jnp.int32, (96, 96), 1)

    def fine_row(i):
        return ((i >> 1) & 1) * 48 + (i & 1) * 24 + (i >> 3) * 2 + ((i >> 2) & 1)

    gather = jnp.where(c96 == fine_row(r96), 1.0, 0.0).astype(BF16)
    scatter = jnp.where(r96 == fine_row(c96), 1.0, 0.0).astype(BF16)

    loads[0].wait()
    wide = jnp.concatenate(
        [
            jnp.concatenate([res[4 * xc + xi] for xi in range(4)], axis=1)
            for xc in range(2)
        ],
        axis=0,
    )
    sorted_rows = dot(wide, perm[...]).astype(BF16)
    for zq in range(4):
        send_in[zq] = sorted_rows[:, 128 * zq : 128 * zq + 128]

    pl.semaphore_wait(barrier, len(greeted))

    def exchange(src, dst, send_sem, recv_sem):
        copies = []
        for j in (2, 3, 1):
            slot = (q + j) % 4
            copy = pltpu.make_async_remote_copy(
                src_ref=src.at[slot],
                dst_ref=dst.at[q],
                send_sem=send_sem.at[j - 1],
                recv_sem=recv_sem.at[j - 1],
                device_id=(base + slot, xy),
                device_id_type=MESH,
            )
            copy.start()
            copies.append(copy)
        dst[pl.ds(q, 1)] = src[pl.ds(q, 1)]
        return copies

    copies_in = exchange(send_in, recv_in, in_send, in_recv)
    lane192 = lanes(192)
    row192 = lax.broadcasted_iota(jnp.int32, (192, 128), 0)
    lane24 = lanes(24)
    row24 = lax.broadcasted_iota(jnp.int32, (24, 128), 0)
    widen = jnp.where((lane24 >> 2) == row24, 1.0, 0.0).astype(BF16)
    loads[3].wait()
    blocks = jnp.where(((row192 ^ lane192) & 3) == 0, dot(inv[...], widen), 0.0).astype(BF16)
    blocks = blocks[:, :96]
    loads[2].wait()
    for pack in range(2):
        placed = jnp.zeros((192, 128), F32)
        for m in range(4):
            shift = jnp.where(lane24 - row24 == 32 * m, 1.0, 0.0).astype(BF16)
            placed = placed + dot(hop[4 * pack + m], shift)
        placed = placed.astype(BF16)
        made = dot(blocks, jnp.concatenate([placed[:96], placed[96:]], axis=1))
        link = jnp.concatenate(
            [made[:96, :128] - made[96:, 128:], made[:96, 128:] + made[96:, :128]], axis=0
        )
        high = link.astype(BF16)
        links[pack, 0] = high
        links[pack, 1] = (link - high.astype(F32)).astype(BF16)
    loads[1].wait()
    pending = list(copies_in)
    for copy in copies_in:
        copy.wait_recv()

    lane96 = lanes(96)
    low96 = lane96 < 64
    gathered = [dot(gather, recv_in[ti]) for ti in range(4)]
    turned = [pltpu.roll(g, 64, 1) for g in gathered]
    halves = []
    for yc in range(2):
        blocks = []
        for h in range(2):
            if yc == 0:
                blocks.append(jnp.where(low96, gathered[2 * h], turned[2 * h + 1]))
            else:
                blocks.append(jnp.where(low96, turned[2 * h], gathered[2 * h + 1]))
        halves.append(
            jnp.concatenate(
                [blocks[h][8 * c : 8 * c + 8] for c in range(12) for h in range(2)], axis=1
            )
        )
    fine = jnp.concatenate(halves, axis=0).astype(BF16)
    fine = jnp.concatenate([fine] * 8, axis=0)
    products = dot_nt(vec[...], fine)

    def part_of(p):
        return own_site(lambda s: products[24 * (2 * s + p) : 24 * (2 * s + p) + 24], lane24)

    rhs = part_of(0) - times_i(part_of(1), lane24)

    def collapse(acc, keep):
        picked = jnp.where((lane96 & 32) == 0, acc[:96], acc[96:])
        if keep:
            picked = jnp.where(low96, picked, 0.0)
        rows_ref[...] = picked
        return spread_groups(own_site(lambda s: rows_ref[pl.ds(s, 24, stride=4)], lane24))

    started = collapse(dot(inv[...], split_field(rhs, lane24).astype(BF16)), True)
    solution = started
    for sweep in range(2):
        plain = split_field(solution, lane24)
        w = jnp.where(lane24 < 64, plain, swap(plain, lane24, 2))
        wide_w = jnp.concatenate([w, jnp.zeros((8, 128), F32)], axis=0)
        halo_out[sweep] = wide_w.astype(BF16)
        copies = {}
        routes = [(5, (ta, x_up)), (4, (ta, x_down)), (0, (t_down, xy))]
        if n_t > 2:
            routes.append((1, (t_up, xy)))
        routes += [(2, (base + (q + 3) % 4, xy)), (3, (base + (q + 1) % 4, xy))]
        for slot, device in routes:
            copy = pltpu.make_async_remote_copy(
                src_ref=halo_out.at[sweep],
                dst_ref=halo_in.at[sweep, slot],
                send_sem=halo_send.at[sweep, slot],
                recv_sem=halo_recv.at[sweep, slot],
                device_id=device,
                device_id_type=MESH,
            )
            copy.start()
            copies[slot] = copy
        flipped = pad_rows(swap(plain, lane24, 8))
        slots = [0, 0 if n_t == 2 else 1, 2, 3]
        for slot in (2, 3) + ((0,) if n_t == 2 else (0, 1)):
            copies[slot].wait_recv()
        near = jnp.concatenate([halo_in[sweep, slot] for slot in slots], axis=0)
        acc = dot(links[0, 0], near) + dot(links[0, 1], near)
        copies[4].wait_recv()
        copies[5].wait_recv()
        first_x = (lanes(32) & 2) == 0
        above = jnp.where(first_x, wide_w, halo_in[sweep, 4].astype(F32)).astype(BF16)
        below = jnp.where(first_x, halo_in[sweep, 5].astype(F32), wide_w).astype(BF16)
        far = jnp.concatenate([above, below, flipped, flipped], axis=0)
        acc_far = dot(links[1, 0], far) + dot(links[1, 1], far)
        acc = jnp.where(lane192 < 64, acc, acc_far)
        solution = started - collapse(acc, False)
        pending += list(copies.values())

    rounded = solution.astype(BF16).astype(F32)
    rotated = times_i(rounded, lane24)
    site = (lane24 & 2) + ((lane24 >> 3) & 1)
    columns = jnp.concatenate(
        [jnp.where(site == s, part, 0.0) for s in range(4) for part in (rounded, rotated)], axis=0
    ).astype(BF16)
    pick = (lax.broadcasted_iota(jnp.int32, (16, 128), 0) == lanes(16)).astype(F32).astype(BF16)
    coefficients = dot_nt(pick, columns).astype(BF16)
    spread = dot(coefficients, vec[...])
    for h in range(2):
        straight = []
        for yc in range(2):
            straight.append(
                jnp.concatenate(
                    [
                        spread[8 * yc : 8 * yc + 8, 256 * c + 128 * h : 256 * c + 128 * h + 128]
                        for c in range(12)
                    ],
                    axis=0,
                )
            )
        crossed = [pltpu.roll(s, 64, 1) for s in straight]
        send_back[2 * h] = jnp.where(low96, straight[0], crossed[1]).astype(BF16)
        send_back[2 * h + 1] = jnp.where(low96, crossed[0], straight[1]).astype(BF16)
    copies_back = exchange(send_back, recv_back, back_send, back_recv)
    pending += copies_back
    for copy in copies_back:
        copy.wait_recv()
    returned = jnp.concatenate(
        [dot(scatter, recv_back[zq]).astype(BF16) for zq in range(4)], axis=1
    )
    result = dot_nt(returned, perm[...]).astype(BF16)
    for xc in range(2):
        for xi in range(4):
            out_ref[4 * xc + xi] = result[48 * xc : 48 * xc + 48, 128 * xi : 128 * xi + 128]
    for copy in pending:
        copy.wait_send()


def shards(n_ta, n_xy, residual, vectors, hopping, inverse):
    res = residual[0].transpose(0, 1, 3, 2, 4).reshape(8, 48, 128)
    vec = vectors.reshape(192, 3072)
    hop = hopping[:, :, :, :, 0, :, 0, :].transpose(0, 1, 2, 4, 5, 3).reshape(8, 192, 24)
    inv = inverse[:, :, :, 0, :, 0, :].transpose(0, 1, 3, 4, 2).reshape(192, 24)
    out = pl.pallas_call(
        functools.partial(kernel, n_ta, n_xy),
        out_shape=jax.ShapeDtypeStruct((8, 48, 128), BF16),
        in_specs=[pl.BlockSpec(memory_space=pltpu.HBM)] * 4,
        out_specs=pl.BlockSpec(memory_space=pltpu.VMEM),
        scratch_shapes=[
            pltpu.VMEM((8, 48, 128), BF16),
            pltpu.VMEM((192, 3072), BF16),
            pltpu.VMEM((8, 192, 24), BF16),
            pltpu.VMEM((192, 24), BF16),
            pltpu.VMEM((512, 512), BF16),
            pltpu.VMEM((4, 96, 128), BF16),
            pltpu.VMEM((4, 96, 128), BF16),
            pltpu.VMEM((2, 32, 128), BF16),
            pltpu.VMEM((2, 6, 32, 128), BF16),
            pltpu.VMEM((4, 96, 128), BF16),
            pltpu.VMEM((4, 96, 128), BF16),
            pltpu.VMEM((2, 2, 192, 128), BF16),
            pltpu.VMEM((96, 128), F32),
            pltpu.SemaphoreType.DMA((4,)),
            pltpu.SemaphoreType.DMA((3,)),
            pltpu.SemaphoreType.DMA((3,)),
            pltpu.SemaphoreType.DMA((2, 6)),
            pltpu.SemaphoreType.DMA((2, 6)),
            pltpu.SemaphoreType.DMA((3,)),
            pltpu.SemaphoreType.DMA((3,)),
        ],
        compiler_params=pltpu.CompilerParams(
            collective_id=0, has_side_effects=True, vmem_limit_bytes=63 * 1024 * 1024
        ),
    )(res, vec, hop, inv)
    return out.astype(F32).reshape(1, 8, 2, 12, 2, 128).transpose(0, 1, 2, 4, 3, 5)


def solution(mesh):
    placed = (
        P("ta", "xy", None, None, None, None),
        P("ta", "xy", None, None, None, None, None),
        P(None, None, None, None, "ta", "xy", None, None),
        P(None, None, None, "ta", "xy", None, None),
    )
    return jax.shard_map(
        functools.partial(shards, mesh.shape["ta"], mesh.shape["xy"]),
        mesh=mesh,
        in_specs=placed,
        out_specs=P("ta", "xy", None, None, None, None),
        check_vma=False,
    )
```

```python
import functools

import jax
import jax.numpy as jnp
from jax import lax
from jax.experimental import pallas as pl
from jax.experimental.pallas import tpu as pltpu
from jax.sharding import PartitionSpec as P

F32 = jnp.float32
BF16 = jnp.bfloat16
NT = (((1,), (1,)), ((), ()))
MESH = pl.DeviceIdType.MESH


def dot(a, b):
    return jnp.dot(a, b, preferred_element_type=F32)


def dot_nt(a, b):
    return lax.dot_general(a, b, NT, preferred_element_type=F32)


def lanes(rows):
    return lax.broadcasted_iota(jnp.int32, (rows, 128), 1)


def ahead(x, by):
    return pltpu.roll(x, 128 - by, 1)


def behind(x, by):
    return pltpu.roll(x, by, 1)


def swap(x, lane, bit):
    return jnp.where((lane & bit) == 0, ahead(x, bit), behind(x, bit))


def times_i(x, lane):
    return jnp.where((lane & 4) == 0, -ahead(x, 4), behind(x, 4))


def own_site(x_of_site, lane):
    site = (lane & 2) + ((lane >> 3) & 1)
    total = jnp.where(site == 0, x_of_site(0), 0.0)
    for s in range(1, 4):
        total = total + jnp.where(site == s, x_of_site(s), 0.0)
    return total


def spread_groups(x):
    for by in (64, 32, 16):
        x = x + pltpu.roll(x, by, 1)
    return x


def split_field(v, lane):
    high = v.astype(BF16).astype(F32)
    base = jnp.where((lane & 16) == 0, high, v - high)
    return jnp.where((lane & 32) == 0, base, times_i(base, lane))


def pad_rows(w):
    return jnp.concatenate([w, jnp.zeros((8, 128), F32)], axis=0).astype(BF16)


def kernel(
    n_ta,
    n_xy,
    res_hbm,
    vec_hbm,
    hop_hbm,
    inv_hbm,
    out_ref,
    res,
    vec,
    hop,
    inv,
    perm,
    send_in,
    recv_in,
    halo_out,
    halo_in,
    send_back,
    recv_back,
    links,
    rows_ref,
    load_sem,
    in_send,
    in_recv,
    halo_send,
    halo_recv,
    back_send,
    back_recv,
):
    ta = lax.axis_index("ta")
    xy = lax.axis_index("xy")
    q = ta % 4
    base = ta - q
    n_t = n_ta // 4

    t_up = (ta + 4) % n_ta
    t_down = (ta + n_ta - 4) % n_ta
    x_up = (xy + 1) % n_xy
    x_down = (xy + n_xy - 1) % n_xy
    beside = q + 1 - 2 * (q % 2)
    slots_of_mates = ((q + 2) % 4, (beside + 2) % 4, beside)
    mates = [base + slot for slot in slots_of_mates]
    greeted = [(mate, xy) for mate in mates] + [(ta, x_up), (ta, x_down), (t_up, xy)]
    if n_t > 2:
        greeted.append((t_down, xy))
    barrier = pltpu.get_barrier_semaphore()
    for device in greeted:
        pl.semaphore_signal(barrier, inc=1, device_id=device, device_id_type=MESH)

    loads = [
        pltpu.make_async_copy(src, dst, load_sem.at[i])
        for i, (src, dst) in enumerate(((res_hbm, res), (vec_hbm, vec), (hop_hbm, hop), (inv_hbm, inv)))
    ]
    loads[0].start()

    row128 = lax.broadcasted_iota(jnp.int32, (128, 128), 0)
    col128 = lanes(128)
    target = (row128 >> 5) * 128 + ((row128 >> 2) & 1) * 64 + ((row128 >> 3) & 3) * 16 + (row128 & 3)
    offset = target - col128
    for xi in range(4):
        for zq in range(4):
            perm[128 * xi : 128 * xi + 128, 128 * zq : 128 * zq + 128] = jnp.where(
                offset == 128 * zq - 4 * xi, 1.0, 0.0
            ).astype(BF16)
    r96 = lax.broadcasted_iota(jnp.int32, (96, 96), 0)
    c96 = lax.broadcasted_iota(jnp.int32, (96, 96), 1)

    def fine_row(i):
        return ((i >> 1) & 1) * 48 + (i & 1) * 24 + (i >> 3) * 2 + ((i >> 2) & 1)

    gather = jnp.where(c96 == fine_row(r96), 1.0, 0.0).astype(BF16)
    scatter = jnp.where(r96 == fine_row(c96), 1.0, 0.0).astype(BF16)

    loads[0].wait()
    for copy in (loads[3], loads[2], loads[1]):
        copy.start()
    wide = jnp.concatenate(
        [
            jnp.concatenate([res[4 * xc + xi] for xi in range(4)], axis=1)
            for xc in range(2)
        ],
        axis=0,
    )
    sorted_rows = dot(wide, perm[...]).astype(BF16)
    for zq in range(4):
        send_in[zq] = sorted_rows[:, 128 * zq : 128 * zq + 128]

    pl.semaphore_wait(barrier, len(greeted))

    def exchange(src, dst, send_sem, recv_sem):
        copies = []
        for j, slot in enumerate(slots_of_mates):
            copy = pltpu.make_async_remote_copy(
                src_ref=src.at[slot],
                dst_ref=dst.at[q],
                send_sem=send_sem.at[j],
                recv_sem=recv_sem.at[j],
                device_id=(base + slot, xy),
                device_id_type=MESH,
            )
            copy.start()
            copies.append(copy)
        dst[pl.ds(q, 1)] = src[pl.ds(q, 1)]
        return copies

    copies_in = exchange(send_in, recv_in, in_send, in_recv)
    lane192 = lanes(192)
    row192 = lax.broadcasted_iota(jnp.int32, (192, 128), 0)
    lane24 = lanes(24)
    row24 = lax.broadcasted_iota(jnp.int32, (24, 128), 0)
    widen = jnp.where((lane24 >> 2) == row24, 1.0, 0.0).astype(BF16)
    loads[3].wait()
    blocks = jnp.where(((row192 ^ lane192) & 3) == 0, dot(inv[...], widen), 0.0).astype(BF16)
    blocks = blocks[:, :96]
    loads[2].wait()
    for pack in range(2):
        placed = jnp.zeros((192, 128), F32)
        for m in range(4):
            shift = jnp.where(lane24 - row24 == 32 * m, 1.0, 0.0).astype(BF16)
            placed = placed + dot(hop[4 * pack + m], shift)
        placed = placed.astype(BF16)
        made = dot(blocks, jnp.concatenate([placed[:96], placed[96:]], axis=1))
        link = jnp.concatenate(
            [made[:96, :128] - made[96:, 128:], made[:96, 128:] + made[96:, :128]], axis=0
        )
        high = link.astype(BF16)
        links[pack, 0] = high
        links[pack, 1] = (link - high.astype(F32)).astype(BF16)
    loads[1].wait()
    pending = list(copies_in)
    for copy in copies_in:
        copy.wait_recv()

    lane96 = lanes(96)
    low96 = lane96 < 64
    gathered = [dot(gather, recv_in[ti]) for ti in range(4)]
    turned = [pltpu.roll(g, 64, 1) for g in gathered]
    halves = []
    for yc in range(2):
        blocks = []
        for h in range(2):
            if yc == 0:
                blocks.append(jnp.where(low96, gathered[2 * h], turned[2 * h + 1]))
            else:
                blocks.append(jnp.where(low96, turned[2 * h], gathered[2 * h + 1]))
        halves.append(
            jnp.concatenate(
                [blocks[h][8 * c : 8 * c + 8] for c in range(12) for h in range(2)], axis=1
            )
        )
    fine = jnp.concatenate(halves, axis=0).astype(BF16)
    fine = jnp.concatenate([fine] * 8, axis=0)
    products = dot_nt(vec[...], fine)

    def part_of(p):
        return own_site(lambda s: products[24 * (2 * s + p) : 24 * (2 * s + p) + 24], lane24)

    rhs = part_of(0) - times_i(part_of(1), lane24)

    def collapse(acc, keep):
        picked = jnp.where((lane96 & 32) == 0, acc[:96], acc[96:])
        if keep:
            picked = jnp.where(low96, picked, 0.0)
        rows_ref[...] = picked
        return spread_groups(own_site(lambda s: rows_ref[pl.ds(s, 24, stride=4)], lane24))

    started = collapse(dot(inv[...], split_field(rhs, lane24).astype(BF16)), True)
    solution = started
    for sweep in range(2):
        plain = split_field(solution, lane24)
        w = jnp.where(lane24 < 64, plain, swap(plain, lane24, 2))
        wide_w = jnp.concatenate([w, jnp.zeros((8, 128), F32)], axis=0)
        halo_out[sweep] = wide_w.astype(BF16)
        copies = {}
        routes = [(5, (ta, x_up)), (4, (ta, x_down)), (0, (t_down, xy))]
        if n_t > 2:
            routes.append((1, (t_up, xy)))
        routes += [(2, (base + (q + 3) % 4, xy)), (3, (base + (q + 1) % 4, xy))]
        for slot, device in routes:
            copy = pltpu.make_async_remote_copy(
                src_ref=halo_out.at[sweep],
                dst_ref=halo_in.at[sweep, slot],
                send_sem=halo_send.at[sweep, slot],
                recv_sem=halo_recv.at[sweep, slot],
                device_id=device,
                device_id_type=MESH,
            )
            copy.start()
            copies[slot] = copy
        flipped = pad_rows(swap(plain, lane24, 8))
        slots = [0, 0 if n_t == 2 else 1, 2, 3]
        for slot in (2, 3) + ((0,) if n_t == 2 else (0, 1)):
            copies[slot].wait_recv()
        near = jnp.concatenate([halo_in[sweep, slot] for slot in slots], axis=0)
        acc = dot(links[0, 0], near) + dot(links[0, 1], near)
        copies[4].wait_recv()
        copies[5].wait_recv()
        first_x = (lanes(32) & 2) == 0
        above = jnp.where(first_x, wide_w, halo_in[sweep, 4].astype(F32)).astype(BF16)
        below = jnp.where(first_x, halo_in[sweep, 5].astype(F32), wide_w).astype(BF16)
        far = jnp.concatenate([above, below, flipped, flipped], axis=0)
        acc_far = dot(links[1, 0], far) + dot(links[1, 1], far)
        acc = jnp.where(lane192 < 64, acc, acc_far)
        solution = started - collapse(acc, False)
        pending += list(copies.values())

    rounded = solution.astype(BF16).astype(F32)
    rotated = times_i(rounded, lane24)
    site = (lane24 & 2) + ((lane24 >> 3) & 1)
    columns = jnp.concatenate(
        [jnp.where(site == s, part, 0.0) for s in range(4) for part in (rounded, rotated)], axis=0
    ).astype(BF16)
    pick = (lax.broadcasted_iota(jnp.int32, (16, 128), 0) == lanes(16)).astype(F32).astype(BF16)
    coefficients = dot_nt(pick, columns).astype(BF16)
    spread = dot(coefficients, vec[...])
    for h in range(2):
        straight = []
        for yc in range(2):
            straight.append(
                jnp.concatenate(
                    [
                        spread[8 * yc : 8 * yc + 8, 256 * c + 128 * h : 256 * c + 128 * h + 128]
                        for c in range(12)
                    ],
                    axis=0,
                )
            )
        crossed = [pltpu.roll(s, 64, 1) for s in straight]
        send_back[2 * h] = jnp.where(low96, straight[0], crossed[1]).astype(BF16)
        send_back[2 * h + 1] = jnp.where(low96, crossed[0], straight[1]).astype(BF16)
    copies_back = exchange(send_back, recv_back, back_send, back_recv)
    pending += copies_back
    for copy in copies_back:
        copy.wait_recv()
    returned = jnp.concatenate(
        [dot(scatter, recv_back[zq]).astype(BF16) for zq in range(4)], axis=1
    )
    result = dot_nt(returned, perm[...])
    for xc in range(2):
        for xi in range(4):
            out_ref[4 * xc + xi] = result[48 * xc : 48 * xc + 48, 128 * xi : 128 * xi + 128]
    for copy in pending:
        copy.wait_send()


def shards(n_ta, n_xy, residual, vectors, hopping, inverse):
    res = residual[0].transpose(0, 1, 3, 2, 4).reshape(8, 48, 128)
    vec = vectors.reshape(192, 3072)
    hop = hopping[:, :, :, :, 0, :, 0, :].transpose(0, 1, 2, 4, 5, 3).reshape(8, 192, 24)
    inv = inverse[:, :, :, 0, :, 0, :].transpose(0, 1, 3, 4, 2).reshape(192, 24)
    out = pl.pallas_call(
        functools.partial(kernel, n_ta, n_xy),
        out_shape=pltpu.VMEM((8, 48, 128), F32),
        in_specs=[pl.BlockSpec(memory_space=pltpu.HBM)] * 4,
        out_specs=pl.BlockSpec(memory_space=pltpu.VMEM),
        scratch_shapes=[
            pltpu.VMEM((8, 48, 128), BF16),
            pltpu.VMEM((192, 3072), BF16),
            pltpu.VMEM((8, 192, 24), BF16),
            pltpu.VMEM((192, 24), BF16),
            pltpu.VMEM((512, 512), BF16),
            pltpu.VMEM((4, 96, 128), BF16),
            pltpu.VMEM((4, 96, 128), BF16),
            pltpu.VMEM((2, 32, 128), BF16),
            pltpu.VMEM((2, 6, 32, 128), BF16),
            pltpu.VMEM((4, 96, 128), BF16),
            pltpu.VMEM((4, 96, 128), BF16),
            pltpu.VMEM((2, 2, 192, 128), BF16),
            pltpu.VMEM((96, 128), F32),
            pltpu.SemaphoreType.DMA((4,)),
            pltpu.SemaphoreType.DMA((3,)),
            pltpu.SemaphoreType.DMA((3,)),
            pltpu.SemaphoreType.DMA((2, 6)),
            pltpu.SemaphoreType.DMA((2, 6)),
            pltpu.SemaphoreType.DMA((3,)),
            pltpu.SemaphoreType.DMA((3,)),
        ],
        compiler_params=pltpu.CompilerParams(
            collective_id=0, has_side_effects=True, vmem_limit_bytes=56 * 1024 * 1024
        ),
    )(res, vec, hop, inv)
    return out.reshape(1, 8, 2, 12, 2, 128).transpose(0, 1, 2, 4, 3, 5)


def solution(mesh):
    placed = (
        P("ta", "xy", None, None, None, None),
        P("ta", "xy", None, None, None, None, None),
        P(None, None, None, None, "ta", "xy", None, None),
        P(None, None, None, "ta", "xy", None, None),
    )
    return jax.shard_map(
        functools.partial(shards, mesh.shape["ta"], mesh.shape["xy"]),
        mesh=mesh,
        in_specs=placed,
        out_specs=P("ta", "xy", None, None, None, None),
        check_vma=False,
    )
```
